256 devices in a mesh: ctx: 32 (over y, z_lo, core), head: 8 (over x, z_hi).
Axes of the slice: x: 4, y: 4, z: 8 (z_hi: 2, z_lo: 4; z = z_hi * 4 + z_lo), core: 2. Of those that a mesh axis runs over, the one named last changes fastest.
Arguments:
- queries: bfloat16 [16384, 4096], P(('ctx', 'head')), may hold values from -3 to 3
- key_states: bfloat16 [16384, 1024], P(('ctx', 'head')), may hold values from -3 to 3
- value_states: bfloat16 [16384, 1024], P(('ctx', 'head')), may hold values from -4 to 4
- outputs: bfloat16 [16384, 4096], P(('ctx', 'head')), may hold values from -4 to 4
- out_grad: bfloat16 [16384, 4096], P(('ctx', 'head')), may hold values from -8 to 8
- log_sums: float32 [16384, 32], P('ctx', 'head'), may hold values from 6 to 9
- selected: int32 [32, 8, 8], P('ctx', 'head'), may hold values from -1 to 31, as said below
Outputs:
- query_grad: bfloat16 [16384, 4096], P(('ctx', 'head'))
- key_grad: bfloat16 [16384, 1024], P(('ctx', 'head'))
- value_grad: bfloat16 [16384, 1024], P(('ctx', 'head'))
The draws below stay inside these ranges and needn't reach their ends.
Inputs may be any that keep to these rules, and one draw needn't show every extreme that they name: selected[c, g, 0] is c, the span's own block; the other entries of a list are distinct blocks earlier than c, chosen more often among early blocks, and -1 marks an empty entry; span c has min(8, c + 1) entries that are not -1.
All inputs are finite; a program needn't handle non-finite values.
Results may differ from the reference program's by a relative error of at most 0.0049.
Values may be sent and summed in bfloat16 or wider, within the bound.
No kernel may reach another device: no remote copies, remote signals or barrier semaphores. Data moves between devices by JAX's collectives and lax.ppermute only.
A program may use at most 192 MiB of HBM per device.

```python
import jax
import jax.numpy as jnp
from jax import lax

DH = 128
KVH = 8
HQG = 4
BLOCK = 512
TOPK = 8
HQ = 32
S = 16384
NB = 32


def draw_selected(key, part):
    key = jax.random.fold_in(key, 11)
    span_ids = jnp.arange(NB, dtype=jnp.int32)[:, None, None]
    block_ids = jnp.arange(NB, dtype=jnp.int32)[None, None, :]
    random_part = jax.random.randint(key, (NB, KVH, NB), 0, 4 * NB, dtype=jnp.int32)
    ranking = (random_part - 3 * block_ids) * NB + (NB - 1 - block_ids)
    earlier = block_ids < span_ids
    ranking = jnp.where(earlier, ranking + 16 * NB * NB, -1).astype(jnp.int32)
    top_score, top_index = lax.top_k(ranking, TOPK - 1)
    others = jnp.where(top_score >= 0, top_index.astype(jnp.int32), -1).astype(jnp.int32)
    own_block = jnp.broadcast_to(span_ids, (NB, KVH, 1)).astype(jnp.int32)
    return jnp.concatenate([own_block, others], axis=-1).astype(jnp.int32)


def shard_levels(key, shape, shards, least, largest):
    level, own = 1.0, jax.random.fold_in(key, 6)
    for axis_at, parts in shards:
        heights = jnp.exp(jax.random.uniform(jax.random.fold_in(own, axis_at), (parts,), jnp.float32, least / len(shards), largest / len(shards)))
        level = level * jnp.repeat(heights, shape[axis_at] // parts).reshape([-1 if axis == axis_at else 1 for axis in range(len(shape))])
    return level


def scatter_about(stream_key, shape, width, reach, pieces=(), kind=jnp.bfloat16):
    drawn = jax.random.normal(stream_key, shape, jnp.float32) * width
    if len(pieces) > 0:
        drawn = shard_levels(stream_key, shape, pieces, -0.22, 0.18) * drawn
    return jnp.clip(drawn, min=-reach, max=reach).astype(kind)


def setup_inputs(seed: int = 0) -> dict:
    key_of = jax.random.split(jax.random.key(seed), 8)
    return {
        "queries": scatter_about(key_of[0], (S, HQ * DH), 1.0, 3.0, ((0, 256),)),
        "key_states": scatter_about(key_of[1], (S, KVH * DH), 1.0, 3.0, ((0, 256),)),
        "value_states": scatter_about(key_of[2], (S, KVH * DH), 1.0, 4.0, ((0, 256),)),
        "outputs": scatter_about(key_of[3], (S, HQ * DH), 1.0, 4.0, ((0, 256),)),
        "out_grad": scatter_about(key_of[4], (S, HQ * DH), 2.0, 8.0, ((0, 256),)),
        "log_sums": jnp.clip(6.0 + 3.0 * jax.random.uniform(key_of[5], (S, HQ), jnp.float32) ** shard_levels(key_of[5], (S, HQ), ((0, 32), (1, 8)), -0.2, 0.2), 6.0, 9.0),
        "selected": draw_selected(jax.random.fold_in(key_of[7], 71), 0),
    }


def span_group(flat_index, query_blocks, output_blocks, grad_blocks, lse_blocks, key_groups, value_groups, selected):
    span_id = flat_index // KVH
    group_id = flat_index % KVH
    score_scale = DH ** -0.5
    query_here = query_blocks[span_id, :, group_id].astype(jnp.float32)
    output_here = output_blocks[span_id, :, group_id].astype(jnp.float32)
    grad_here = grad_blocks[span_id, :, group_id].astype(jnp.float32)
    lse_here = lse_blocks[span_id, :, group_id]
    slot_ids = selected[span_id, group_id]
    live_slot = slot_ids >= 0
    safe_slot = jnp.where(live_slot, slot_ids, 0)
    key_index = (safe_slot[:, None] * BLOCK + jnp.arange(BLOCK, dtype=jnp.int32)[None, :]).reshape(-1)
    key_live = jnp.repeat(live_slot, BLOCK)
    query_pos = span_id * BLOCK + jnp.arange(BLOCK, dtype=jnp.int32)
    allowed = key_live[None, :] & (key_index[None, :] <= query_pos[:, None])
    keys_here = key_groups[:, group_id][key_index].astype(jnp.float32)
    values_here = value_groups[:, group_id][key_index].astype(jnp.float32)
    scores = jnp.einsum("qhd,kd->hqk", query_here, keys_here) * score_scale
    weights = jnp.where(allowed[None], jnp.exp(scores - lse_here.T[:, :, None]), 0.0)
    probs_low = lax.optimization_barrier(weights.astype(jnp.bfloat16)).astype(jnp.float32)
    grad_probs = jnp.einsum("qhd,kd->hqk", grad_here, values_here)
    row_delta = jnp.sum(grad_here * output_here, axis=-1)
    grad_scores = weights * (grad_probs - row_delta.T[:, :, None])
    grad_low = lax.optimization_barrier(grad_scores.astype(jnp.bfloat16)).astype(jnp.float32)
    query_part = jnp.einsum("hqk,kd->qhd", grad_low, keys_here) * score_scale
    key_part = (jnp.einsum("hqk,qhd->kd", grad_low, query_here) * score_scale).reshape(TOPK, BLOCK, DH)
    value_part = jnp.einsum("hqk,qhd->kd", probs_low, grad_here).reshape(TOPK, BLOCK, DH)
    return query_part, key_part, value_part


def reference(queries, key_states, value_states, outputs, out_grad, log_sums, selected):
    query_blocks = queries.reshape(NB, BLOCK, KVH, HQG, DH)
    output_blocks = outputs.reshape(NB, BLOCK, KVH, HQG, DH)
    grad_blocks = out_grad.reshape(NB, BLOCK, KVH, HQG, DH)
    lse_blocks = log_sums.reshape(NB, BLOCK, KVH, HQG)
    key_groups = key_states.reshape(S, KVH, DH)
    value_groups = value_states.reshape(S, KVH, DH)

    def per_pair(flat_index):
        return span_group(flat_index, query_blocks, output_blocks, grad_blocks, lse_blocks, key_groups, value_groups, selected)

    query_all, key_slots, value_slots = lax.map(per_pair, jnp.arange(NB * KVH, dtype=jnp.int32))
    query_grad = query_all.reshape(NB, KVH, BLOCK, HQG, DH).transpose(0, 2, 1, 3, 4).reshape(S, HQ * DH).astype(jnp.bfloat16)
    target = jnp.where(selected >= 0, selected, NB).astype(jnp.int32)
    group_ids = jnp.broadcast_to(jnp.arange(KVH, dtype=jnp.int32)[None, :, None], selected.shape)
    key_dense = jnp.zeros((NB, KVH, BLOCK, DH), jnp.float32).at[target, group_ids].add(key_slots.reshape(NB, KVH, TOPK, BLOCK, DH), mode="drop")
    value_dense = jnp.zeros((NB, KVH, BLOCK, DH), jnp.float32).at[target, group_ids].add(value_slots.reshape(NB, KVH, TOPK, BLOCK, DH), mode="drop")
    key_grad = key_dense.transpose(0, 2, 1, 3).reshape(S, KVH * DH).astype(jnp.bfloat16)
    value_grad = value_dense.transpose(0, 2, 1, 3).reshape(S, KVH * DH).astype(jnp.bfloat16)
    return (query_grad, key_grad, value_grad)
```

```python
import functools

import jax
import jax.numpy as jnp
from jax import lax
from jax.experimental import pallas as pl
from jax.experimental.pallas import tpu as pltpu
from jax.sharding import Mesh, PartitionSpec as P

DH = 128
HQG = 4
BLOCK = 512
TOPK = 8
GROUPS = 8
NB = 32
SHARD = 64
CHUNK = 128
ROWS = 512
KEYS = 512
SCALE = DH ** (-0.5)
LOG2E = 1.4426950408889634
ZH = ("z", "h")
ZCH = ("z", "c", "h")
PLANE = ("y", "c", "x")
OFFSETS = (0, 1, -1, 2)
BF = jnp.bfloat16
F32 = jnp.float32


def plane_index(y, c, x):
    return ((y % 4) * 2 + c) * 4 + (x % 4)


def shift(array, phase, distance):
    pairs = []
    for y in range(4):
        for c in range(2):
            for x in range(4):
                along_x = (c == 0) == (phase == 0)
                target = plane_index(y, c, x + distance) if along_x else plane_index(y + distance, c, x)
                pairs.append((plane_index(y, c, x), target))
    return lax.ppermute(array, PLANE, pairs)


def swap(array):
    return lax.ppermute(array, "c", [(0, 1), (1, 0)])


def spread(own):
    first = [own] + [shift(own, 0, -d) for d in OFFSETS[1:]]
    row = jnp.concatenate(first, axis=0)
    mine = [row] + [shift(row, 1, -d) for d in OFFSETS[1:]]
    return mine, [swap(m) for m in mine]


def total(*terms):
    return functools.reduce(lambda a, b: a + b, [t.astype(F32) for t in terms])


def ring_sum(own, plus, minus, far, phase):
    half = far.shape[0] // 2
    low = shift(far[:half], phase, 1)
    high = shift(far[half:], phase, -1)
    plus = jnp.concatenate(
        [total(*[p[:half] for p in plus], low), total(*[p[half:] for p in plus])], axis=0
    )
    minus = jnp.concatenate(
        [total(*[m[:half] for m in minus]), total(*[m[half:] for m in minus], high)], axis=0
    )
    got_plus = shift(plus.astype(BF), phase, 1)
    got_minus = shift(minus.astype(BF), phase, -1)
    return total(*own, got_plus, got_minus)


def gather_sums(theirs_far, theirs_near, mine_far, mine_near):
    far = total(mine_far, swap(theirs_far)).astype(BF)
    size = far.shape[0]
    near = [mine_near, swap(theirs_near)]
    cut = lambda i: [a[i * size : (i + 1) * size] for a in near]
    part = ring_sum(cut(0), cut(1), cut(2), far, 0)
    size //= 4
    cut = lambda i: part[i * size : (i + 1) * size]
    return ring_sum([cut(0)], [cut(1)], [cut(2)], cut(3).astype(BF), 1).astype(BF)


def kernel(
    meta, chosen, lse_ref, delta_ref, qdo_ref,
    w0, w1, w2, w3, o0, o1, o2, o3,
    theirs_far, theirs_near, mine_far, mine_near, dq_ref,
    kv, acc, q_t, do_t, dq_t, sems,
):
    x, y, core = meta[0], meta[1], meta[2]

    def place(owner_core, d1, d2):
        on_x = owner_core == 0
        return (
            lax.rem(x + jnp.where(on_x, d1, d2) + 4, 4),
            lax.rem(y + jnp.where(on_x, d2, d1) + 4, 4),
        )

    copies = []
    for which, refs in ((core, (w0, w1, w2, w3)), (1 - core, (o0, o1, o2, o3))):
        for i2, ref in enumerate(refs):
            for i1 in range(4):
                xb, yb = place(which, OFFSETS[i1], OFFSETS[i2])
                copy = pltpu.make_async_copy(
                    ref.at[pl.ds(i1 * 8, 8)],
                    kv.at[which, pl.ds(yb * 8, 8), pl.ds(pl.multiple_of(xb * CHUNK, CHUNK), CHUNK)],
                    sems.at[0],
                )
                copy.start()
                copies.append(copy)

    def clear(i, _):
        acc[0, i] = jnp.zeros((BLOCK, DH), F32)
        acc[1, i] = jnp.zeros((BLOCK, DH), F32)
        return 0

    lax.fori_loop(0, NB, clear, 0)
    for copy in copies:
        copy.wait()

    def span(s, _):
        q = qdo_ref[pl.ds(2 * s, 2), 0:256, :].reshape(ROWS, DH)
        do = qdo_ref[pl.ds(2 * s, 2), 256:512, :].reshape(ROWS, DH)
        q_t[...] = q.T
        do_t[...] = do.T
        dq_t[...] = jnp.zeros((DH, ROWS), F32)
        slot_row = lax.rem(x - s + 4, 4)
        lse = lse_ref[slot_row] * LOG2E
        delta = delta_ref[s]

        def tile(block, start, own):
            keys = kv[0, block, start : start + KEYS, :]
            values = kv[1, block, start : start + KEYS, :]
            scores = jnp.dot(keys, q_t[...], preferred_element_type=F32)
            probs = jnp.exp2(scores * (SCALE * LOG2E) - lse)
            if own:
                key_at = start + lax.broadcasted_iota(jnp.int32, (KEYS, ROWS), 0)
                row = lax.broadcasted_iota(jnp.int32, (KEYS, ROWS), 1)
                query_at = x * CHUNK + (row // 256) * SHARD + lax.rem(row, SHARD)
                probs = jnp.where(key_at <= query_at, probs, 0.0)
            grad_probs = jnp.dot(values, do_t[...], preferred_element_type=F32)
            grad_low = (probs * (grad_probs - delta)).astype(BF)
            acc[1, block, start : start + KEYS, :] += jnp.dot(
                probs.astype(BF), qdo_ref[pl.ds(2 * s, 2), 256:512, :].reshape(ROWS, DH), preferred_element_type=F32
            )
            acc[0, block, start : start + KEYS, :] += jnp.dot(
                grad_low, qdo_ref[pl.ds(2 * s, 2), 0:256, :].reshape(ROWS, DH), preferred_element_type=F32
            )
            dq_t[...] += lax.dot_general(
                keys, grad_low, (((0,), (0,)), ((), ())), preferred_element_type=F32
            )

        own_block = chosen[slot_row, 0]
        for start in range(0, BLOCK, KEYS):
            tile(own_block, start, True)

        def slot(r, _):
            block = chosen[slot_row, r]

            @pl.when(block >= 0)
            def _():
                for start in range(0, BLOCK, KEYS):
                    tile(block, start, False)

            return 0

        lax.fori_loop(1, TOPK, slot, 0)
        dq = (dq_t[...] * SCALE).T.astype(BF)
        dq_ref[pl.ds(2 * s, 2)] = dq.reshape(2, 256, DH)
        return 0

    lax.fori_loop(0, 4, span, 0)

    for which, near, far in ((core, mine_near, mine_far), (1 - core, theirs_near, theirs_far)):
        factor = jnp.where(which == 0, SCALE, 1.0).astype(F32)
        for i1 in range(4):
            for i2 in range(4):
                xb, yb = place(which, OFFSETS[i1], OFFSETS[i2])
                piece = acc[which, pl.ds(yb * 8, 8), pl.ds(pl.multiple_of(xb * CHUNK, CHUNK), CHUNK), :]
                piece = (piece * factor).astype(BF)
                if i1 == 3:
                    far[pl.ds(i2 * 8, 8)] = piece
                else:
                    near[pl.ds((i1 * 4 + i2) * 8, 8)] = piece


def attend(meta, chosen, lse, delta, qdo, mine, other):
    vmem = pl.BlockSpec(memory_space=pltpu.VMEM)
    smem = pl.BlockSpec(memory_space=pltpu.SMEM)
    hbm = pl.BlockSpec(memory_space=pl.ANY)
    shape = jax.ShapeDtypeStruct
    return pl.pallas_call(
        kernel,
        out_shape=(
            shape((32, CHUNK, DH), BF),
            shape((96, CHUNK, DH), BF),
            shape((32, CHUNK, DH), BF),
            shape((96, CHUNK, DH), BF),
            shape((8, 256, DH), BF),
        ),
        in_specs=[smem, smem, vmem, vmem, vmem] + [hbm] * 8,
        out_specs=(vmem,) * 5,
        scratch_shapes=[
            pltpu.VMEM((2, NB, BLOCK, DH), BF),
            pltpu.VMEM((2, NB, BLOCK, DH), F32),
            pltpu.VMEM((DH, ROWS), BF),
            pltpu.VMEM((DH, ROWS), BF),
            pltpu.VMEM((DH, ROWS), F32),
            pltpu.SemaphoreType.DMA((1,)),
        ],
        compiler_params=pltpu.CompilerParams(vmem_limit_bytes=56 * 1024 * 1024),
        cost_estimate=pl.CostEstimate(flops=20 * 10**9, bytes_accessed=20 * 2**20, transcendentals=0),
        name="attend",
    )(meta, chosen, lse, delta, qdo, *mine, *other)


def by_group(array):
    return array.reshape(SHARD, GROUPS, -1, DH).transpose(1, 2, 0, 3)


def from_groups(array):
    return array.transpose(2, 0, 1, 3).reshape(SHARD, -1)


def split_three(array):
    high = lax.reduce_precision(array, 8, 7)
    rest = array - high
    middle = lax.reduce_precision(rest, 8, 7)
    low = rest - middle
    return jnp.stack([high.astype(BF), middle.astype(BF), low.astype(BF)], axis=1)


def shards(queries, key_states, value_states, outputs, out_grad, log_sums, selected):
    x, y, c = lax.axis_index("x"), lax.axis_index("y"), lax.axis_index("c")
    meta = jnp.stack([x, y, c]).astype(jnp.int32)

    keys, values = by_group(key_states), by_group(value_states)
    kv_send = jnp.stack([keys, values], axis=1).reshape(4, 2, 2, SHARD, DH).transpose(0, 2, 1, 3, 4)
    kv_own = lax.all_to_all(kv_send.reshape(16, SHARD, DH), ZCH, split_axis=0, concat_axis=0, tiled=True)
    mine, other = spread(kv_own.reshape(1024, DH))
    mine = [m.reshape(32, CHUNK, DH) for m in mine]
    other = [m.reshape(32, CHUNK, DH) for m in other]

    lse_send = log_sums.reshape(4, 2, SHARD, HQG).transpose(0, 1, 3, 2).reshape(4, ROWS)
    chosen_send = jnp.broadcast_to(selected.reshape(1, TOPK).astype(F32), (4, TOPK))
    small = jnp.concatenate([lse_send, jnp.pad(chosen_send, ((0, 0), (0, 128 - TOPK)))], axis=1)
    z = lax.axis_index("z")
    pieces = []
    for d in range(4):
        piece = lax.dynamic_index_in_dim(small, lax.rem(z + d, 4), 0, keepdims=False)
        pairs = [(zl * 4 + xh, xh * 4 + (zl + d) % 4) for zl in range(4) for xh in range(4)]
        pieces.append(lax.ppermute(piece, ("z", "x"), pairs))
    small = jnp.stack(pieces)
    lse = small[:, :ROWS].reshape(4, 1, ROWS)
    chosen = small[:, ROWS : ROWS + TOPK].astype(jnp.int32)

    delta = jnp.sum(
        (out_grad.astype(F32) * outputs.astype(F32)).reshape(SHARD, GROUPS * HQG, DH), axis=-1
    )
    delta = delta.T.reshape(GROUPS, HQG * SHARD)
    delta_rows = jnp.pad(split_three(delta).reshape(GROUPS, 6, DH), ((0, 0), (0, 10), (0, 0)))
    qdo_send = jnp.concatenate(
        [by_group(queries).reshape(GROUPS, 256, DH), by_group(out_grad).reshape(GROUPS, 256, DH), delta_rows],
        axis=1,
    )
    qdo = lax.all_to_all(qdo_send, ZH, split_axis=0, concat_axis=0, tiled=True)
    delta = jnp.sum(qdo[:, 512:518, :].reshape(8, 3, 256).astype(F32), axis=1).reshape(4, 1, ROWS)

    theirs_far, theirs_near, mine_far, mine_near, dq = attend(meta, chosen, lse, delta, qdo, mine, other)
    flat = lambda a: a.reshape(-1, DH)
    kv_grad = gather_sums(flat(theirs_far), flat(theirs_near), flat(mine_far), flat(mine_near))
    query_grad = lax.all_to_all(dq, ZH, split_axis=0, concat_axis=0, tiled=True)
    kv_grad = lax.all_to_all(kv_grad.reshape(16, SHARD, DH), ZCH, split_axis=0, concat_axis=0, tiled=True)
    kv_grad = kv_grad.reshape(4, 2, 2, SHARD, DH)
    return (
        from_groups(query_grad.reshape(GROUPS, HQG, SHARD, DH)),
        from_groups(kv_grad[:, 0].reshape(GROUPS, 1, SHARD, DH)),
        from_groups(kv_grad[:, 1].reshape(GROUPS, 1, SHARD, DH)),
    )


def solution(mesh):
    wide = Mesh(mesh.devices.reshape(4, 4, 2, 4, 2), ("y", "z", "c", "x", "h"))
    rows = P(("y", "z", "c", "x", "h"), None)
    return jax.shard_map(
        shards,
        mesh=wide,
        in_specs=(
            rows,
            rows,
            rows,
            rows,
            rows,
            P(("y", "z", "c"), ("x", "h")),
            P(("y", "z", "c"), ("x", "h"), None),
        ),
        out_specs=(rows, rows, rows),
        check_vma=False,
    )
```

```python
import functools

import jax
import jax.numpy as jnp
from jax import lax
from jax.experimental import pallas as pl
from jax.experimental.pallas import tpu as pltpu
from jax.sharding import Mesh, PartitionSpec as P

DH = 128
HQG = 4
BLOCK = 512
TOPK = 8
GROUPS = 8
HELD = 16
EXTRA = 32
SHARD = 64
CHUNK = 128
ROWS = 512
UNROLL = 2
SCALE = DH ** (-0.5)
LOG2E = 1.4426950408889634
ZH = ("z", "h")
PLANE = ("y", "c", "x")
OFFSETS = (0, 1, -1, 2)
BF = jnp.bfloat16
F32 = jnp.float32


def plane_index(y, c, x):
    return ((y % 4) * 2 + c) * 4 + (x % 4)


def shift(array, phase, distance):
    pairs = []
    for y in range(4):
        for c in range(2):
            for x in range(4):
                along_x = (c == 0) == (phase == 0)
                target = plane_index(y, c, x + distance) if along_x else plane_index(y + distance, c, x)
                pairs.append((plane_index(y, c, x), target))
    return lax.ppermute(array, PLANE, pairs)


def swap(array):
    return lax.ppermute(array, "c", [(0, 1), (1, 0)])


def tie(first, *rest):
    return lax.optimization_barrier((first, *rest))


def after(array, *others):
    return lax.optimization_barrier((array, *others))[0]


def round_the_ring(array, phase):
    return [shift(array, phase, -d) for d in OFFSETS[1:]]


def kernel(
    meta, chosen, lse_ref, delta_ref, qdo_own, qdo_other, w0, w1, w2, w3,
    own_ref, plus_ref, minus_ref, far_ref, dq_own, dq_other,
    qdo, kv, acc, dq_t, items, sems,
):
    x, y, core = meta[0], meta[1], meta[2]

    def place(d1, d2):
        on_x = core == 0
        return (
            lax.rem(x + jnp.where(on_x, d1, d2) + 4, 4),
            lax.rem(y + jnp.where(on_x, d2, d1) + 4, 4),
        )

    copies = [
        pltpu.make_async_copy(ref, qdo.at[i], sems.at[0]) for i, ref in enumerate((qdo_own, qdo_other))
    ]
    for i2, ref in enumerate((w0, w1, w2, w3)):
        for i1 in range(4):
            xb, yb = place(OFFSETS[i1], OFFSETS[i2])
            copies.append(pltpu.make_async_copy(ref.at[i1], kv.at[pl.ds(yb * 4, 4), xb], sems.at[0]))
    for copy in copies:
        copy.start()

    def clear(i, _):
        acc[i] = jnp.zeros(acc.shape[1:], F32)
        return 0

    lax.fori_loop(0, HELD, clear, 0)
    dq_t[...] = jnp.zeros_like(dq_t)

    def span_q(e):
        return qdo[e // 4, pl.ds(2 * lax.rem(e, 4), 2), 0:256, :].reshape(ROWS, DH)

    def span_do(e):
        return qdo[e // 4, pl.ds(2 * lax.rem(e, 4), 2), 256:512, :].reshape(ROWS, DH)

    def listing(i, count):
        e = i // (TOPK - 1)
        block = chosen[e, 1 + lax.rem(i, TOPK - 1)]
        take = jnp.logical_and(block >= 0, lax.rem(block, 2) == core)
        items[count] = e * 64 + block // 2
        return count + take.astype(jnp.int32)

    count = lax.fori_loop(0, 8 * (TOPK - 1), listing, jnp.int32(0))
    for i in range(UNROLL):
        items[count + i] = jnp.int32(0)
    for copy in copies:
        copy.wait()

    def item(e, block, own, live):
        keys = kv[block, :, :, 0].reshape(BLOCK, DH)
        values = kv[block, :, :, 1].reshape(BLOCK, DH)
        q, do = span_q(e), span_do(e)
        lse = lse_ref[e] * LOG2E
        if live is not None:
            lse = lse + jnp.where(live, 0.0, 1e30)
        last = (((1,), (1,)), ((), ()))
        scores = lax.dot_general(keys, q, last, preferred_element_type=F32)
        probs = jnp.exp2(scores * (SCALE * LOG2E) - lse)
        if own:
            key_at = lax.broadcasted_iota(jnp.int32, (BLOCK, ROWS), 0)
            row = lax.broadcasted_iota(jnp.int32, (BLOCK, ROWS), 1)
            query_at = x * CHUNK + (row // 256) * SHARD + lax.rem(row, SHARD)
            probs = jnp.where(key_at <= query_at, probs, 0.0)
        grad_probs = lax.dot_general(values, do, last, preferred_element_type=F32)
        grad_low = (probs * (grad_probs - delta_ref[e])).astype(BF)
        split = lambda a: a.reshape(4, 2, SHARD, DH)
        acc[block, :, :, 1] += split(jnp.dot(probs.astype(BF), do, preferred_element_type=F32))
        acc[block, :, :, 0] += split(jnp.dot(grad_low, q, preferred_element_type=F32))
        dq_t[e] += lax.dot_general(keys, grad_low, (((0,), (0,)), ((), ())), preferred_element_type=F32)

    for s in range(4):
        item(s, chosen[s, 0] // 2, True, None)

    def some(i, _):
        for u in range(UNROLL):
            at = i * UNROLL + u
            code = items[at]
            item(code // 64, lax.rem(code, 64), False, None if u == 0 else at < count)
        return 0

    lax.fori_loop(0, (count + UNROLL - 1) // UNROLL, some, 0)

    for i1, ref in ((3, far_ref), (1, plus_ref), (2, minus_ref), (0, own_ref)):
        for i2 in range(4):
            xb, yb = place(OFFSETS[i1], OFFSETS[i2])
            piece = acc[pl.ds(yb * 4, 4), xb]
            ref[i2, :, :, 0] = (piece[:, :, 0] * SCALE).astype(ref.dtype)
            ref[i2, :, :, 1] = piece[:, :, 1].astype(ref.dtype)

    def finish(s, _):
        dq_own[pl.ds(2 * s, 2)] = (dq_t[s] * SCALE).T.reshape(2, 256, DH)
        dq_other[pl.ds(2 * s, 2)] = (dq_t[s + 4] * SCALE).T.reshape(2, 256, DH)
        return 0

    lax.fori_loop(0, 4, finish, 0)


def attend(meta, chosen, lse, delta, qdo_own, qdo_other, rows):
    vmem = pl.BlockSpec(memory_space=pltpu.VMEM)
    smem = pl.BlockSpec(memory_space=pltpu.SMEM)
    hbm = pl.BlockSpec(memory_space=pl.ANY)
    shape = jax.ShapeDtypeStruct
    chunk = (4, 4, 2, 2, SHARD, DH)
    return pl.pallas_call(
        kernel,
        out_shape=(shape(chunk, F32),) + (shape(chunk, BF),) * 3 + (shape((8, 256, DH), F32),) * 2,
        in_specs=[smem, smem, vmem, vmem] + [hbm] * 6,
        out_specs=(vmem,) * 6,
        scratch_shapes=[
            pltpu.VMEM((2, GROUPS, ROWS + EXTRA, DH), BF),
            pltpu.VMEM((HELD, 4, 2, 2, SHARD, DH), BF),
            pltpu.VMEM((HELD, 4, 2, 2, SHARD, DH), F32),
            pltpu.VMEM((8, DH, ROWS), F32),
            pltpu.SMEM((64,), jnp.int32),
            pltpu.SemaphoreType.DMA((1,)),
        ],
        compiler_params=pltpu.CompilerParams(vmem_limit_bytes=56 * 1024 * 1024),
        cost_estimate=pl.CostEstimate(flops=20 * 10**9, bytes_accessed=20 * 2**20, transcendentals=0),
        name="attend",
    )(meta, chosen, lse, delta, qdo_own, qdo_other, *rows)


def by_group(array):
    return array.reshape(SHARD, GROUPS, -1, DH).transpose(1, 2, 0, 3)


def from_groups(array):
    return array.transpose(2, 0, 1, 3).reshape(SHARD, -1)


def split_three(array):
    high = lax.reduce_precision(array, 8, 7)
    rest = array - high
    middle = lax.reduce_precision(rest, 8, 7)
    low = rest - middle
    return jnp.stack([high.astype(BF), middle.astype(BF), low.astype(BF)], axis=1)


def shards(queries, key_states, value_states, outputs, out_grad, log_sums, selected):
    x, y, c = lax.axis_index("x"), lax.axis_index("y"), lax.axis_index("c")
    meta = jnp.stack([x, y, c]).astype(jnp.int32)

    kv_send = jnp.concatenate([by_group(key_states), by_group(value_states)], axis=1)

    lse = log_sums.reshape(4, 2, SHARD, HQG).transpose(0, 1, 3, 2).reshape(4, ROWS)
    chosen = jnp.broadcast_to(selected.reshape(1, TOPK).astype(F32), (4, TOPK))
    small = jnp.concatenate([lse, jnp.pad(chosen, ((0, 0), (0, 128 - TOPK)))], axis=1)
    kv_send, small = tie(kv_send, small)
    chunk = lambda d: lax.dynamic_index_in_dim(small, lax.rem(x + d, 4), 0, keepdims=False)
    move = lambda d: lax.ppermute(chunk(d), "x", [(i, (i + d) % 4) for i in range(4)])
    pieces = [chunk(0), move(3), move(2), move(1)]
    small = lax.dynamic_slice(jnp.stack(pieces + pieces), (lax.rem(4 - x, 4), 0), (4, ROWS + 128))
    lse_rows = split_three(small[:, :ROWS]).reshape(4, 12, DH)
    chosen_rows = small[:, ROWS:].astype(BF).reshape(4, 1, DH)
    small_rows = jnp.concatenate([lse_rows, chosen_rows], axis=1).reshape(4, 1, 13, DH)
    same = jnp.arange(2).reshape(1, 2, 1, 1) == lax.axis_index("h")
    small_rows = jnp.where(same, small_rows, 0).reshape(GROUPS, 13, DH)

    kv_own = lax.all_to_all(kv_send, ZH, split_axis=0, concat_axis=0, tiled=True)

    delta = jnp.sum(
        (out_grad.astype(F32) * outputs.astype(F32)).reshape(SHARD, GROUPS * HQG, DH), axis=-1
    )
    delta = delta.T.reshape(GROUPS, HQG * SHARD)
    delta_rows = split_three(delta).reshape(GROUPS, 6, DH)
    extra = [delta_rows, small_rows, jnp.zeros((GROUPS, EXTRA - 19, DH), BF)]
    (extra,) = tie(jnp.concatenate(extra, axis=1))
    qdo_send = jnp.concatenate(
        [by_group(queries).reshape(GROUPS, 256, DH), by_group(out_grad).reshape(GROUPS, 256, DH), extra],
        axis=1,
    )
    own = kv_own.reshape(1, 4, 2, 2, SHARD, DH)
    first = round_the_ring(own, 0)
    qdo_send = after(qdo_send, *first)
    qdo = lax.all_to_all(qdo_send, ZH, split_axis=0, concat_axis=0, tiled=True)
    row = jnp.concatenate([own] + first, axis=0)
    rows = [row] + round_the_ring(row, 1)

    qdo = after(qdo, *rows[1:])
    qdo_other = swap(qdo)
    extra = jnp.stack([qdo[:, ROWS:], qdo_other[:, ROWS:]]).reshape(8, 2, EXTRA, DH).astype(F32)
    delta = jnp.sum(extra[:, :, :6].reshape(8, 2, 3, 256), axis=2).reshape(8, 1, ROWS)
    extra = lax.dynamic_index_in_dim(extra, lax.axis_index("h"), 1, keepdims=False)
    lse = jnp.sum(extra[:, 6:18].reshape(8, 3, ROWS), axis=1).reshape(8, 1, ROWS)
    chosen = extra[:, 18, :TOPK].astype(jnp.int32)

    own, plus, minus, far, dq_own, dq_other = attend(meta, chosen, lse, delta, qdo, qdo_other, rows)
    dq = (dq_own + swap(dq_other)).astype(BF)
    query_grad = lax.all_to_all(dq, ZH, split_axis=0, concat_axis=0, tiled=True)
    part = sum([shift(a, 0, d).astype(F32) for a, d in ((far, 2), (plus, 1), (minus, -1))], own)
    part = after(part, query_grad)
    got = [shift(part[i].astype(BF), 1, d).astype(F32) for i, d in ((3, 2), (1, 1), (2, -1))]
    kv_grad = sum(got, part[0]).astype(BF).reshape(GROUPS, 2, SHARD, DH)
    kv_grad = lax.all_to_all(kv_grad, ZH, split_axis=0, concat_axis=0, tiled=True)
    return (
        from_groups(query_grad.reshape(GROUPS, HQG, SHARD, DH)),
        from_groups(kv_grad[:, :1]),
        from_groups(kv_grad[:, 1:]),
    )


def solution(mesh):
    wide = Mesh(mesh.devices.reshape(4, 4, 2, 4, 2), ("y", "z", "c", "x", "h"))
    rows = P(("y", "z", "c", "x", "h"), None)
    return jax.shard_map(
        shards,
        mesh=wide,
        in_specs=(
            rows,
            rows,
            rows,
            rows,
            rows,
            P(("y", "z", "c"), ("x", "h")),
            P(("y", "z", "c"), ("x", "h"), None),
        ),
        out_specs=(rows, rows, rows),
        check_vma=False,
    )
```
